128 devices in a mesh: view: 16 (over z, x), img: 8 (over y, core).
Axes of the slice: x: 4, y: 4, z: 4, core: 2. Of those that a mesh axis runs over, the one named last changes fastest.
Arguments:
- volume: bfloat16 [256, 256, 2048], P('view', 'img'), may hold values from -6 to 6
- occupied: int32 [16, 8, 16], P('view', 'img'), may hold values from -1 to 15, as said below
- sample_counts: int32 [16, 8, 16], P('view', 'img'), may hold values from 6 to 24, as said below
- depth_order: int32 [16], replicated, may hold values from 0 to 15, each once
- colors: bfloat16 [3, 128], replicated, may hold values from 0.049804688 to 1
- density: bfloat16 [128], replicated, may hold values from 0.0019989014 to 0.039794922
Outputs:
- frame: float32 [4, 256, 2048], P(None, 'img', 'view')
The draws below stay inside these ranges and needn't reach their ends.
Inputs may be any that keep to these rules, and one draw needn't show every extreme that they name: `occupied`: each brick's list names distinct tiles of 0..15 first and then holds -1; a brick lists 16, half, a quarter or an eighth of its tiles (at least 2), and some brick lists all of them. `sample_counts`: every brick has a tile with 24 samples. `depth_order`: A permutation of the bricks along view.
All inputs are finite; a program needn't handle non-finite values.
Results may differ from the reference program's by a relative error of at most 0.0003.
Values may be sent and summed in bfloat16 or wider, within the bound.
No kernel may reach another device: no remote copies, remote signals or barrier semaphores. Data moves between devices by JAX's collectives and lax.ppermute only.
A program may use at most 64 MiB of HBM per device.

```python
import math
import jax
import jax.numpy as jnp
from jax import lax

SLICES = 16
ROWS = 32
COLS = 2048
TILE_COLS = 128
SAMPLE_MAX = 24
BINS = 128
SAMPLE_MIN = 6
TILES_DEV = 16
DEPTH = 256
FRAME_ROWS = 256
N_VIEW = 16
N_IMG = 8


def draw_occupied(key, part):
    bricks = N_VIEW * N_IMG
    key_drop, key_full, key_order = jax.random.split(jax.random.fold_in(key, 101), 3)
    halvings = jax.random.randint(key_drop, (bricks,), 0, 4)
    fullest = jax.random.randint(key_full, (), 0, bricks)
    halvings = jnp.where(jnp.arange(bricks) == fullest, 0, halvings)
    listed_count = jnp.maximum(jnp.right_shift(jnp.int32(TILES_DEV), halvings), 2)
    shuffled = jax.vmap(lambda inner: jax.random.permutation(inner, TILES_DEV))(jax.random.split(key_order, bricks))
    chosen = jnp.where(jnp.arange(TILES_DEV)[None, :] < listed_count[:, None], shuffled, -1)
    return chosen.reshape(N_VIEW, N_IMG, TILES_DEV).astype(jnp.int32)


def draw_sample_counts(key, part):
    bricks = N_VIEW * N_IMG
    key_count, key_top = jax.random.split(jax.random.fold_in(key, 202))
    drawn = jax.random.randint(key_count, (bricks, TILES_DEV), SAMPLE_MIN, SAMPLE_MAX + 1)
    topmost = jax.random.randint(key_top, (bricks, 1), 0, TILES_DEV)
    drawn = jnp.where(jnp.arange(TILES_DEV)[None, :] == topmost, SAMPLE_MAX, drawn)
    return drawn.reshape(N_VIEW, N_IMG, TILES_DEV).astype(jnp.int32)


def level_of(stream_key, extent, cuts, low, largest):
    factor_of, own = 1.0, jax.random.fold_in(stream_key, 6)
    for dim, shards_of in cuts:
        steps = jnp.exp(jax.random.uniform(jax.random.fold_in(own, dim), (shards_of,), jnp.float32, low / len(cuts), largest / len(cuts)))
        factor_of = factor_of * jnp.repeat(steps, extent[dim] // shards_of).reshape([-1 if axis == dim else 1 for axis in range(len(extent))])
    return factor_of


def normal_values(own_key, extent, spread, reach, shards=(), held_as=jnp.bfloat16):
    values = jax.random.normal(own_key, extent, jnp.float32) * spread
    if len(shards) > 0:
        values = level_of(own_key, extent, shards, -0.22, 0.18) * values
    return jnp.clip(values, min=-reach, max=reach).astype(held_as)


def setup_inputs(seed: int = 0) -> dict:
    key_list = jax.random.split(jax.random.key(seed), 7)
    volume = normal_values(key_list[0], (DEPTH, FRAME_ROWS, COLS), 1.0, 6.0, ((0, 16), (1, 8)))
    occupied = draw_occupied(jax.random.fold_in(key_list[6], 71), 0)
    sample_counts = draw_sample_counts(jax.random.fold_in(key_list[6], 71), 0)
    depth_order = jax.random.permutation(key_list[3], N_VIEW).astype(jnp.int32)
    colors = jnp.clip(jax.random.uniform(key_list[4], (3, BINS), jnp.float32, 0.049804688, 1.0), 0.049804688, 1.0).astype(jnp.bfloat16)
    density = jnp.clip(jnp.exp(jax.random.uniform(key_list[5], (BINS,), jnp.float32, math.log(0.0019989014), math.log(0.039794922))), 0.0019989014, 0.039794922).astype(jnp.bfloat16)
    return dict(volume=volume, occupied=occupied, sample_counts=sample_counts, depth_order=depth_order, colors=colors, density=density)


def tent(offset):
    return jnp.maximum(0.0, 1.0 - jnp.abs(offset))


def reference(volume, occupied, sample_counts, depth_order, colors, density):
    table = jnp.concatenate([colors, density[None, :]], axis=0)
    zero_slice = jnp.zeros((1, FRAME_ROWS, COLS), volume.dtype)
    padded = jnp.pad(jnp.concatenate([volume, zero_slice], axis=0), ((0, 0), (1, 1), (1, 1)))
    tile_of_column = jnp.arange(COLS, dtype=jnp.int32) // TILE_COLS
    slice_index = jnp.arange(SLICES + 1, dtype=jnp.float32)
    bin_index = jnp.arange(BINS, dtype=jnp.float32)[:, None]
    tile_index = jnp.arange(TILES_DEV, dtype=jnp.int32)

    def march_brick(brick):
        view_pos = (brick // N_IMG).astype(jnp.int32)
        group_pos = (brick % N_IMG).astype(jnp.int32)
        anchor = jnp.zeros((), jnp.int32)
        cube = lax.dynamic_slice(padded, ((view_pos * SLICES).astype(jnp.int32), (group_pos * ROWS).astype(jnp.int32), anchor), (SLICES + 1, ROWS + 2, COLS + 2)).astype(jnp.float32)
        across = (cube[:, 2:, 1:-1] - cube[:, :-2, 1:-1]) * 0.5
        along = (cube[:, 1:-1, 2:] - cube[:, 1:-1, :-2]) * 0.5
        grads = across * across + along * along
        values = cube[:, 1:-1, 1:-1]
        listed = lax.dynamic_slice(occupied, (view_pos, group_pos, anchor), (1, 1, TILES_DEV))[0, 0]
        counted = lax.dynamic_slice(sample_counts, (view_pos, group_pos, anchor), (1, 1, TILES_DEV))[0, 0]
        present = jnp.any(listed[None, :] == tile_index[:, None], axis=1)
        column_count = counted[tile_of_column]
        column_live = present[tile_of_column]
        count_float = column_count.astype(jnp.float32)

        def sample(carry, number):
            paint, cover, remain = carry
            position = (number.astype(jnp.float32) + 1.0) * SLICES / count_float
            weights_z = tent(position[None, :] - slice_index[:, None])
            sampled = jnp.einsum("jc,jrc->rc", weights_z, values, precision=lax.Precision.HIGHEST)
            sampled_grad = jnp.einsum("jc,jrc->rc", weights_z, grads, precision=lax.Precision.HIGHEST)
            levels = jax.nn.sigmoid(sampled) * (BINS - 1)
            lookup = tent(levels.reshape(1, -1) - bin_index).astype(jnp.bfloat16)
            looked = jnp.dot(table, lookup, preferred_element_type=jnp.float32).reshape(4, ROWS, COLS)
            shading = 0.4 + 0.6 * sampled_grad / (1.0 + sampled_grad)
            opacity = 1.0 - jnp.exp(-(looked[3] * SLICES / count_float))
            live_now = jnp.logical_and(number < column_count, column_live)
            opacity = jnp.where(live_now[None, :], opacity, 0.0)
            weight = remain * opacity
            paint = paint + weight * shading * looked[0:3]
            cover = cover + weight
            remain = remain * (1.0 - opacity)
            return (paint, cover, remain), None

        start = (jnp.zeros((3, ROWS, COLS), jnp.float32), jnp.zeros((ROWS, COLS), jnp.float32), jnp.ones((ROWS, COLS), jnp.float32))
        finished, unused = lax.scan(sample, start, jnp.arange(SAMPLE_MAX, dtype=jnp.int32))
        return jnp.concatenate([finished[0], finished[1][None]], axis=0)

    partials = lax.map(march_brick, jnp.arange(N_VIEW * N_IMG, dtype=jnp.int32))
    layers = partials.reshape(N_VIEW, N_IMG, 4, ROWS, COLS).transpose(0, 2, 1, 3, 4).reshape(N_VIEW, 4, FRAME_ROWS, COLS)

    def blend(position, carry):
        image, remain = carry
        chosen = lax.dynamic_index_in_dim(layers, depth_order[position], 0, keepdims=False)
        return image + remain[None] * chosen, remain * (1.0 - chosen[3])

    image, remain = lax.fori_loop(0, N_VIEW, blend, (jnp.zeros((4, FRAME_ROWS, COLS), jnp.float32), jnp.ones((FRAME_ROWS, COLS), jnp.float32)))
    return image
```

```python
import jax
import jax.numpy as jnp
from jax import lax
from jax.experimental import pallas as pl
from jax.experimental.pallas import tpu as pltpu
from jax.sharding import PartitionSpec as P

TILE_COLS = 128
GROUP_ROWS = 8
UNROLL = 8
LOG2E = 1.4426950408889634
COLOR_UNIT = 4096.0
DENSITY_UNIT = 65536.0
ENTRY_SHIFT = 18
SENT_UNIT = 131070.0
SENT_ZERO = 32768

LANE_GATHER = lax.GatherDimensionNumbers(
    offset_dims=(),
    collapsed_slice_dims=(1,),
    start_index_map=(1,),
    operand_batching_dims=(0,),
    start_indices_batching_dims=(0,),
)


def looked_up(row, index):
    return lax.gather(
        row,
        index[..., None],
        LANE_GATHER,
        slice_sizes=(1, 1),
        mode=lax.GatherScatterMode.PROMISE_IN_BOUNDS,
    )


def march_kernel(occupied, counts, volume, following, low, high, colors, density, out, values, grads):
    slices, rows, columns = volume.shape
    tiles = columns // TILE_COLS
    groups = rows // GROUP_ROWS
    shape = (GROUP_ROWS, TILE_COLS)
    listed = jnp.int32(0)
    for slot in range(tiles):
        listed = listed + (occupied[slot] >= 0).astype(jnp.int32)
    out[...] = jnp.full(out.shape, -SENT_ZERO, jnp.int16)
    row_of = lax.broadcasted_iota(jnp.int32, (rows, TILE_COLS), 0)
    lane_of = lax.broadcasted_iota(jnp.int32, (rows, TILE_COLS), 1)
    table = []
    for channel in range(4):
        source = colors[channel : channel + 1] if channel < 3 else density[...]
        unit = COLOR_UNIT if channel < 3 else DENSITY_UNIT
        entry = jnp.broadcast_to((source.astype(jnp.float32) * unit).astype(jnp.int32), shape)
        second = pltpu.roll(entry, TILE_COLS - 1, 1)
        table.append((entry << ENTRY_SHIFT) | second)

    def march_tile(slot, carry):
        tile = occupied[slot]
        samples = counts[tile]
        here = pl.multiple_of(tile * TILE_COLS, TILE_COLS)
        before = pl.multiple_of(jnp.maximum(tile - 1, 0) * TILE_COLS, TILE_COLS)
        after = pl.multiple_of(jnp.minimum(tile + 1, tiles - 1) * TILE_COLS, TILE_COLS)
        low_rows = low[:, pl.ds(here, TILE_COLS)].astype(jnp.float32)
        high_rows = high[:, pl.ds(here, TILE_COLS)].astype(jnp.float32)

        def prepared(j):
            def part(start):
                if j < slices:
                    return volume[j, :, pl.ds(start, TILE_COLS)].astype(jnp.float32)
                return following[0, :, pl.ds(start, TILE_COLS)].astype(jnp.float32)

            block = part(here)
            left = jnp.where(tile > 0, part(before), 0.0)
            right = jnp.where(tile < tiles - 1, part(after), 0.0)
            above = jnp.where(row_of == 0, low_rows[j : j + 1], pltpu.roll(block, 1, 0))
            below = jnp.where(row_of == rows - 1, high_rows[j : j + 1], pltpu.roll(block, rows - 1, 0))
            left = pltpu.roll(jnp.where(lane_of == TILE_COLS - 1, left, block), 1, 1)
            right = pltpu.roll(jnp.where(lane_of == 0, right, block), TILE_COLS - 1, 1)
            across = below - above
            along = right - left
            return block * 0.5, (across * across + along * along) * (0.25 / 0.6) + (1.0 / 0.6)

        last = None
        for j in range(slices + 1):
            current = prepared(j)
            values[2 * j] = current[0]
            grads[2 * j] = current[1]
            if j > 0:
                values[2 * j - 1] = current[0] - last[0]
                grads[2 * j - 1] = current[1] - last[1]
            last = current

        spacing = slices / samples.astype(jnp.float32)
        thickness = spacing * (-LOG2E / DENSITY_UNIT)

        def looked(k, group):
            position = jnp.minimum((k + 1).astype(jnp.float32) * spacing, float(slices))
            j = jnp.minimum(position.astype(jnp.int32), slices - 1)
            part = position - j.astype(jnp.float32)
            at = pl.ds(GROUP_ROWS * group, GROUP_ROWS)
            half_value = values[2 * j, at] + part * values[2 * j + 1, at]
            gradient = grads[2 * j, at] + part * grads[2 * j + 1, at]
            level = 63.5 + 63.5 * jnp.tanh(half_value)
            index = level.astype(jnp.int32)
            second = level - index.astype(jnp.float32)
            first = 1.0 - second
            second = second.astype(jnp.bfloat16).astype(jnp.float32)
            first = first.astype(jnp.bfloat16).astype(jnp.float32)
            pairs = [looked_up(row, index) for row in table]
            shade = 1.0 - pl.reciprocal(gradient, approx=True)
            return first, second, shade, pairs

        def composited(k, sample, state):
            first, second, shade, pairs = sample
            thick = jnp.where(k < samples, thickness, 0.0)
            first = first * (1.0 / (1 << ENTRY_SHIFT))
            uppers = [pair.astype(jnp.float32) for pair in pairs]
            lowers = [(pair & ((1 << 13) - 1)).astype(jnp.float32) for pair in pairs]
            red, green, blue, remain = state
            remain_after = remain * jnp.exp2((first * uppers[3] + second * lowers[3]) * thick)
            weight = (remain - remain_after) * shade
            first = weight * first
            second = weight * second
            return (
                red + first * uppers[0] + second * lowers[0],
                green + first * uppers[1] + second * lowers[1],
                blue + first * uppers[2] + second * lowers[2],
                remain_after,
            )

        def march_block(number, states):
            states = list(states)
            base = number * UNROLL
            ready = [[looked(base + u, g) for g in range(groups)] for u in range(UNROLL)]
            for u in range(UNROLL):
                for g in range(groups):
                    states[g] = composited(base + u, ready[u][g], states[g])
            return tuple(states)

        zero = jnp.zeros(shape, jnp.float32)
        start = tuple((zero, zero, zero, jnp.ones(shape, jnp.float32)) for g in range(groups))
        states = lax.fori_loop(0, (samples + UNROLL - 1) // UNROLL, march_block, start)
        for pair in range(groups // 2):
            for channel in range(4):
                both = jnp.concatenate([states[2 * pair][channel], states[2 * pair + 1][channel]], axis=0)
                both = (1.0 - both) * SENT_UNIT if channel == 3 else both * (SENT_UNIT / COLOR_UNIT)
                both = jnp.round(both).astype(jnp.int32) - SENT_ZERO
                out[tile, channel, pl.ds(2 * GROUP_ROWS * pair, 2 * GROUP_ROWS)] = both.astype(jnp.int16)
        return carry

    lax.fori_loop(0, listed, march_tile, 0)


def march(occupied, counts, volume, following, low, high, colors, density):
    slices, rows, columns = volume.shape
    scalars = pl.BlockSpec(memory_space=pltpu.SMEM)
    block = pl.BlockSpec(memory_space=pltpu.VMEM)
    return pl.pallas_call(
        march_kernel,
        out_shape=jax.ShapeDtypeStruct((columns // TILE_COLS, 4, rows, TILE_COLS), jnp.int16),
        in_specs=[scalars] * 2 + [block] * 6,
        out_specs=block,
        scratch_shapes=[pltpu.VMEM((2 * slices + 2, rows, TILE_COLS), jnp.float32)] * 2,
        compiler_params=pltpu.CompilerParams(vmem_limit_bytes=40 * 2**20),
        name="march",
    )(occupied, counts, volume, following, low, high, colors, density)


def blend_kernel(order, layers, out):
    bricks, channels, rows, columns = layers.shape
    for start in range(0, rows, 16):
        at = pl.ds(start, 16)

        def step(position, carry):
            image, remain = carry
            brick = order[position]
            chosen = [
                (layers[brick, c, at].astype(jnp.int32) + SENT_ZERO).astype(jnp.float32) for c in range(channels)
            ]
            image = tuple(image[c] + remain * chosen[c] for c in range(channels))
            return image, remain * (1.0 - chosen[channels - 1] * (1.0 / SENT_UNIT))

        zero = jnp.zeros((16, columns), jnp.float32)
        carry = ((zero,) * channels, jnp.full((16, columns), 1.0 / SENT_UNIT, jnp.float32))
        for position in range(bricks):
            carry = step(position, carry)
        for c in range(channels):
            out[c, at] = carry[0][c]


def blend(order, layers):
    bricks, channels, rows, columns = layers.shape
    block = pl.BlockSpec(memory_space=pltpu.VMEM)
    return pl.pallas_call(
        blend_kernel,
        out_shape=jax.ShapeDtypeStruct((channels, rows, columns), jnp.float32),
        in_specs=[pl.BlockSpec(memory_space=pltpu.SMEM), block],
        out_specs=block,
        compiler_params=pltpu.CompilerParams(vmem_limit_bytes=16 * 2**20),
        name="blend",
    )(order, layers)


def shards(volume, occupied, sample_counts, depth_order, colors, density):
    slices, rows, columns = volume.shape
    bricks = lax.axis_size("view")
    bands = lax.axis_size("img")
    back = [(i + 1, i) for i in range(bricks - 1)]
    down = [(i, i + 1) for i in range(bands - 1)]
    up = [(i + 1, i) for i in range(bands - 1)]
    following = lax.ppermute(volume[0:1], "view", back)
    bottom = jnp.concatenate([volume[:, rows - 1], following[:, rows - 1]], axis=0)
    top = jnp.concatenate([volume[:, 0], following[:, 0]], axis=0)
    low = lax.ppermute(bottom, "img", down)
    high = lax.ppermute(top, "img", up)
    partial = march(
        occupied.reshape(-1), sample_counts.reshape(-1), volume, following, low, high, colors, density[None, :]
    )
    layers = lax.all_to_all(partial, "view", 0, 0, tiled=True)
    return blend(depth_order, layers)


def solution(mesh):
    return jax.shard_map(
        shards,
        mesh=mesh,
        in_specs=(
            P("view", "img", None),
            P("view", "img", None),
            P("view", "img", None),
            P(),
            P(),
            P(),
        ),
        out_specs=P(None, "img", "view"),
        check_vma=False,
    )
```

```python
import functools

import jax
import jax.numpy as jnp
from jax import lax
from jax.experimental import pallas as pl
from jax.experimental.pallas import tpu as pltpu
from jax.sharding import PartitionSpec as P

TILE_COLS = 128
GROUP_ROWS = 8
SENT_ROWS = 48
UNROLL = 12
VMEM_LIMIT = 60 * 2**20
BLEND_LIMIT = 16 * 2**20
UNROLLS = (5, 6, 7, 8, 9, 10, 11, 12)
LOG2E = 1.4426950408889634
COLOR_UNIT = 4096.0
DENSITY_UNIT = 65536.0
ENTRY_SHIFT = 18
SENT_UNIT = 131070.0
SENT_ZERO = 32768

LANE_GATHER = lax.GatherDimensionNumbers(
    offset_dims=(),
    collapsed_slice_dims=(1,),
    start_index_map=(1,),
    operand_batching_dims=(0,),
    start_indices_batching_dims=(0,),
)


def looked_up(row, index):
    return lax.gather(
        row,
        index[..., None],
        LANE_GATHER,
        slice_sizes=(1, 1),
        mode=lax.GatherScatterMode.PROMISE_IN_BOUNDS,
    )


def tile_table(colors, density):
    shape = (GROUP_ROWS, TILE_COLS)
    table = []
    for channel in range(4):
        source = colors[channel : channel + 1] if channel < 3 else density[...]
        unit = COLOR_UNIT if channel < 3 else DENSITY_UNIT
        entry = jnp.broadcast_to((source.astype(jnp.float32) * unit).astype(jnp.int32), shape)
        second = pltpu.roll(entry, TILE_COLS - 1, 1)
        table.append((entry << ENTRY_SHIFT) | second)
    return table


def listed_by_samples(occupied, counts, ordered):
    slots = occupied.shape[0]
    tiles = [occupied[slot] for slot in range(slots)]
    samples = [counts[jnp.maximum(tile, 0)] for tile in tiles]
    keys = [
        jnp.where(tile >= 0, count * slots + slot, slots * 1024 + slot)
        for slot, (tile, count) in enumerate(zip(tiles, samples))
    ]
    listed = jnp.int32(0)
    ranks = [jnp.int32(slot) for slot in range(slots)]
    for slot in range(slots):
        for other in range(slot):
            moved = (keys[slot] < keys[other]).astype(jnp.int32)
            ranks[other] = ranks[other] + moved
            ranks[slot] = ranks[slot] - moved
    for slot in range(slots):
        ordered[ranks[slot]] = tiles[slot]
        listed = listed + (tiles[slot] >= 0).astype(jnp.int32)
    return listed


def samples_before_last(samples, slices):
    return ((slices - 1) * samples) // slices


def neighbours(tile, tiles):
    here = pl.multiple_of(tile * TILE_COLS, TILE_COLS)
    before = pl.multiple_of(jnp.maximum(tile - 1, 0) * TILE_COLS, TILE_COLS)
    after = pl.multiple_of(jnp.minimum(tile + 1, tiles - 1) * TILE_COLS, TILE_COLS)
    return before, here, after


def prepared(load, low_row, high_row, tile, tiles, groups_of, count):
    shape = (GROUP_ROWS, TILE_COLS)
    before, here, after = neighbours(tile, tiles)
    row_of = lax.broadcasted_iota(jnp.int32, shape, 0)
    lane_of = lax.broadcasted_iota(jnp.int32, shape, 1)

    def split(block):
        block = block.astype(jnp.float32)
        return [block[g * GROUP_ROWS : (g + 1) * GROUP_ROWS] for g in range(count)]

    parts, lefts, rights = split(load(here)), split(load(before)), split(load(after))
    result = {}
    for g in groups_of:
        part = parts[g]
        left = jnp.where(tile > 0, lefts[g], 0.0)
        right = jnp.where(tile < tiles - 1, rights[g], 0.0)
        left = pltpu.roll(jnp.where(lane_of == TILE_COLS - 1, left, part), 1, 1)
        right = pltpu.roll(jnp.where(lane_of == 0, right, part), TILE_COLS - 1, 1)
        above = pltpu.roll(parts[g - 1], 1, 0) if g > 0 else jnp.broadcast_to(low_row, shape)
        below = (
            pltpu.roll(parts[g + 1], GROUP_ROWS - 1, 0) if g < count - 1 else jnp.broadcast_to(high_row, shape)
        )
        above = jnp.where(row_of == 0, above, pltpu.roll(part, 1, 0))
        below = jnp.where(row_of == GROUP_ROWS - 1, below, pltpu.roll(part, GROUP_ROWS - 1, 0))
        across = below - above
        along = right - left
        result[g] = part * 0.5, (across * across + along * along) * (0.25 / 0.6) + (1.0 / 0.6)
    return result


def looked(half_value, gradient, table):
    level = 63.5 + 63.5 * jnp.tanh(half_value)
    index = level.astype(jnp.int32)
    second = level - index.astype(jnp.float32)
    first = 1.0 - second
    second = second.astype(jnp.bfloat16).astype(jnp.float32)
    first = first.astype(jnp.bfloat16).astype(jnp.float32)
    pairs = [looked_up(row, index) for row in table]
    shade = 1.0 - pl.reciprocal(gradient, approx=True)
    return first, second, shade, pairs


def composited(thick, sample, state):
    first, second, shade, pairs = sample
    uppers = [pair.astype(jnp.float32) for pair in pairs]
    lowers = [(pair << ENTRY_SHIFT).astype(jnp.float32) for pair in pairs]
    red, green, blue, remain = state
    remain_after = remain * jnp.exp2((first * uppers[3] + second * lowers[3]) * thick)
    weight = (remain - remain_after) * shade
    first = weight * first
    second = weight * second
    return (
        red + first * uppers[0] + second * lowers[0],
        green + first * uppers[1] + second * lowers[1],
        blue + first * uppers[2] + second * lowers[2],
        remain_after,
    )


def march_kernel(groups, edges, *refs):
    there = refs[: 5 + edges]
    out = refs[5 + edges]
    here = refs[6 + edges : 11 + 2 * edges]
    halves, steps, grads, ordered, sems = refs[11 + 2 * edges :]
    occupied, counts, colors, density, cube = here[:5]
    if edges:
        low, high = here[5:]
    slices, rows, columns = there[4].shape
    targets = [*here[:4], cube.at[:, :, pl.ds(TILE_COLS, columns)], *here[5:]]
    copies = [pltpu.make_async_copy(source, target, sems.at[i]) for i, (source, target) in enumerate(zip(there, targets))]
    for copy in copies:
        copy.start()
    for end in (0, columns + TILE_COLS):
        cube[:, :, pl.ds(end, TILE_COLS)] = jnp.zeros((slices, rows, TILE_COLS), cube.dtype)
    tiles = columns // TILE_COLS
    count = rows // GROUP_ROWS
    shape = (GROUP_ROWS, TILE_COLS)
    for copy in copies[:4]:
        copy.wait()
    listed = listed_by_samples(occupied, counts, ordered)
    table = tile_table(colors, density)
    for copy in copies[4:]:
        copy.wait()

    lane_of = lax.broadcasted_iota(jnp.int32, shape, 1)

    def rows_of(g):
        return pl.ds((g + 1) * GROUP_ROWS, GROUP_ROWS)

    def prepare(tile, place):
        at = pl.multiple_of(tile * TILE_COLS, TILE_COLS)
        near = [pl.ds(pl.multiple_of(at + i * TILE_COLS, TILE_COLS), TILE_COLS) for i in range(3)]
        if edges:
            low_rows = low[:, pl.ds(at, TILE_COLS)].astype(jnp.float32) * 0.5
            high_rows = high[:, pl.ds(at, TILE_COLS)].astype(jnp.float32) * 0.5
        last_half, last_gradient = {}, {}
        for j in range(slices):
            left, block, right = [cube[j, :, span].astype(jnp.float32) for span in near]
            if edges:
                halves[place, j, GROUP_ROWS - 1 : GROUP_ROWS] = low_rows[j : j + 1]
                halves[place, j, rows + GROUP_ROWS : rows + GROUP_ROWS + 1] = high_rows[j : j + 1]
            for g in range(count):
                halves[place, j, rows_of(g)] = block[g * GROUP_ROWS : (g + 1) * GROUP_ROWS] * 0.5
            for i, g in enumerate(groups):
                part = slice(g * GROUP_ROWS, (g + 1) * GROUP_ROWS)
                half = block[part] * 0.5
                before = pltpu.roll(jnp.where(lane_of == TILE_COLS - 1, left[part], block[part]), 1, 1)
                after = pltpu.roll(jnp.where(lane_of == 0, right[part], block[part]), TILE_COLS - 1, 1)
                along = after - before
                above = halves[place, j, pl.ds((g + 1) * GROUP_ROWS - 1, GROUP_ROWS)]
                below = halves[place, j, pl.ds((g + 1) * GROUP_ROWS + 1, GROUP_ROWS)]
                across = below - above
                gradient = across * across * (1.0 / 0.6) + (along * along * (0.25 / 0.6) + (1.0 / 0.6))
                grads[place, 2 * j, i] = gradient
                if j > 0:
                    steps[place, j - 1, i] = half - last_half[g]
                    grads[place, 2 * j - 1, i] = gradient - last_gradient[g]
                last_half[g], last_gradient[g] = half, gradient

    def march_two(number, carry):
        two = [ordered[2 * number], ordered[2 * number + 1]]
        marched, spacing, thickness = [], [], []
        for place, tile in enumerate(two):
            samples = counts[tile]
            marched.append(samples_before_last(samples, slices))
            spacing.append(slices / samples.astype(jnp.float32))
            thickness.append(spacing[place] * (-LOG2E / (DENSITY_UNIT * (1 << ENTRY_SHIFT))))
            prepare(tile, place)

        def sampled(k, place):
            position = jnp.minimum((k + 1).astype(jnp.float32) * spacing[place], slices - 1.0)
            j = jnp.minimum(position.astype(jnp.int32), slices - 2)
            part = position - j.astype(jnp.float32)
            return [
                looked(
                    halves[place, j, rows_of(g)] + part * steps[place, j, i],
                    grads[place, 2 * j, i] + part * grads[place, 2 * j + 1, i],
                    table,
                )
                for i, g in enumerate(groups)
            ]

        longest = jnp.maximum(marched[0], marched[1])
        blocks = (longest + UNROLL - 1) // UNROLL
        size = (longest + blocks - 1) // blocks
        chains = [(place, i) for place in range(2) for i in range(len(groups))]

        def march_blocks(unroll):
            def march_block(number, states):
                states = list(states)
                base = number * unroll
                ready = [[sampled(base + u, place) for place in range(2)] for u in range(unroll)]
                for u in range(unroll):
                    thick = [jnp.where(base + u < marched[place], thickness[place], 0.0) for place in range(2)]
                    for c, (place, i) in enumerate(chains):
                        states[c] = composited(thick[place], ready[u][place][i], states[c])
                return tuple(states)

            zero = jnp.zeros(shape, jnp.float32)
            start = tuple((zero, zero, zero, jnp.ones(shape, jnp.float32)) for c in chains)
            states = lax.fori_loop(0, blocks, march_block, start)
            for c, (place, i) in enumerate(chains):
                for channel in range(4):
                    out[two[place], i, channel] = states[c][channel]

        for unroll in UNROLLS:
            at_least = unroll == UNROLLS[0]
            pl.when(size <= unroll if at_least else size == unroll)(functools.partial(march_blocks, unroll))
        return carry

    lax.fori_loop(0, listed // 2, march_two, 0)


def held_here(value):
    space = pltpu.SMEM if value.dtype == jnp.int32 else pltpu.VMEM
    return space(value.shape, value.dtype)


def march(groups, occupied, counts, volume, edges, colors, density):
    slices, rows, columns = volume.shape
    arrays = (occupied, counts, colors, density, volume, *edges)
    tile = (len(groups), GROUP_ROWS, TILE_COLS)
    scratch = [held_here(value) for value in arrays]
    scratch[4] = pltpu.VMEM((slices, rows, columns + 2 * TILE_COLS), volume.dtype)
    return pl.pallas_call(
        functools.partial(march_kernel, groups, len(edges)),
        out_shape=jax.ShapeDtypeStruct(
            (columns // TILE_COLS, len(groups), 4, GROUP_ROWS, TILE_COLS), jnp.float32
        ),
        in_specs=[pl.BlockSpec(memory_space=pl.ANY)] * len(arrays),
        out_specs=pl.BlockSpec(memory_space=pltpu.VMEM),
        scratch_shapes=scratch
        + [
            pltpu.VMEM((2, slices, rows + 2 * GROUP_ROWS, TILE_COLS), jnp.float32),
            pltpu.VMEM((2, slices - 1, *tile), jnp.float32),
            pltpu.VMEM((2, 2 * slices - 1, *tile), jnp.float32),
            pltpu.SMEM(occupied.shape, jnp.int32),
            pltpu.SemaphoreType.DMA((len(arrays),)),
        ],
        compiler_params=pltpu.CompilerParams(vmem_limit_bytes=VMEM_LIMIT),
        cost_estimate=pl.CostEstimate(flops=8_000_000, bytes_accessed=16_000_000, transcendentals=2_000_000),
        name="march_edges" if edges else "march_middle",
    )(*arrays)


def finish_kernel(
    occupied_hbm,
    counts_hbm,
    colors_hbm,
    density_hbm,
    volume_hbm,
    low_hbm,
    high_hbm,
    following_hbm,
    middle_hbm,
    outer_hbm,
    out,
    occupied,
    counts,
    colors,
    density,
    own,
    low,
    high,
    following,
    middle,
    outer,
    sems,
):
    slices, rows, columns = volume_hbm.shape
    tiles = columns // TILE_COLS
    count = rows // GROUP_ROWS
    pairs = [
        (occupied_hbm, occupied),
        (counts_hbm, counts),
        (colors_hbm, colors),
        (density_hbm, density),
        (volume_hbm.at[pl.ds(slices - 1, 1)], own),
        (low_hbm, low),
        (high_hbm, high),
        (following_hbm, following),
        (middle_hbm, middle),
        (outer_hbm, outer),
    ]
    copies = [pltpu.make_async_copy(source, target, sems.at[i]) for i, (source, target) in enumerate(pairs)]
    for copy in copies:
        copy.start()
    out[...] = jnp.full(out.shape, -SENT_ZERO, jnp.int16)
    for copy in copies:
        copy.wait()
    table = tile_table(colors, density)
    listed = jnp.int32(0)
    for slot in range(tiles):
        listed = listed + (occupied[slot] >= 0).astype(jnp.int32)

    def finish_tile(tile):
        samples = counts[tile]
        marched = samples_before_last(samples, slices)
        here = neighbours(tile, tiles)[1]
        groups = tuple(range(count))
        low_rows = low[:, pl.ds(here, TILE_COLS)].astype(jnp.float32)
        high_rows = high[:, pl.ds(here, TILE_COLS)].astype(jnp.float32)
        next_edges = following[rows : rows + 2, pl.ds(here, TILE_COLS)].astype(jnp.float32)
        near = prepared(
            lambda start: own[0, :, pl.ds(start, TILE_COLS)],
            low_rows[slices - 1 : slices],
            high_rows[slices - 1 : slices],
            tile,
            tiles,
            groups,
            count,
        )
        far = prepared(
            lambda start: following[0:rows, pl.ds(start, TILE_COLS)],
            next_edges[0:1],
            next_edges[1:2],
            tile,
            tiles,
            groups,
            count,
        )
        spacing = slices / samples.astype(jnp.float32)
        thickness = spacing * (-LOG2E / (DENSITY_UNIT * (1 << ENTRY_SHIFT)))
        states = []
        for g in groups:
            source, i = (middle, g - 1) if 0 < g < count - 1 else (outer, 0 if g == 0 else 1)
            states.append(tuple(source[tile, i, channel] for channel in range(4)))
        for u in range(2):
            k = marched + u
            part = jnp.minimum((k + 1).astype(jnp.float32) * spacing - (slices - 1.0), 1.0)
            thick = jnp.where(k < samples, thickness, 0.0)
            for g in groups:
                half_value = near[g][0] + part * (far[g][0] - near[g][0])
                gradient = near[g][1] + part * (far[g][1] - near[g][1])
                states[g] = composited(thick, looked(half_value, gradient, table), states[g])
        for pair in range(count // 2):
            for channel in range(4):
                both = jnp.concatenate([states[2 * pair][channel], states[2 * pair + 1][channel]], axis=0)
                if channel == 3:
                    both = (1.0 - both) * SENT_UNIT
                else:
                    both = both * (SENT_UNIT / (COLOR_UNIT * (1 << ENTRY_SHIFT)))
                both = jnp.round(both).astype(jnp.int32) - SENT_ZERO
                out[tile, channel, pl.ds(2 * GROUP_ROWS * pair, 2 * GROUP_ROWS)] = both.astype(jnp.int16)

    def finish_two(number, carry):
        finish_tile(occupied[2 * number])
        finish_tile(occupied[2 * number + 1])
        return carry

    lax.fori_loop(0, listed // 2, finish_two, 0)


def finish(occupied, counts, volume, edges, following, middle, outer, colors, density):
    slices, rows, columns = volume.shape
    arrays = (occupied, counts, colors, density, volume, *edges, following, middle, outer)
    scratch = [held_here(value) for value in arrays]
    scratch[4] = pltpu.VMEM((1, rows, columns), volume.dtype)
    return pl.pallas_call(
        finish_kernel,
        out_shape=jax.ShapeDtypeStruct((columns // TILE_COLS, 4, rows, TILE_COLS), jnp.int16),
        in_specs=[pl.BlockSpec(memory_space=pl.ANY)] * len(arrays),
        out_specs=pl.BlockSpec(memory_space=pltpu.VMEM),
        scratch_shapes=scratch + [pltpu.SemaphoreType.DMA((len(arrays),))],
        compiler_params=pltpu.CompilerParams(vmem_limit_bytes=VMEM_LIMIT),
        name="finish",
    )(*arrays)


def blend_kernel(order, layers, out):
    bricks, channels, rows, columns = layers.shape
    for start in range(0, rows, 16):
        at = pl.ds(start, 16)

        def step(position, carry):
            image, remain = carry
            brick = order[position]
            chosen = [
                (layers[brick, c, at].astype(jnp.int32) + SENT_ZERO).astype(jnp.float32) for c in range(channels)
            ]
            image = tuple(image[c] + remain * chosen[c] for c in range(channels))
            return image, remain * (1.0 - chosen[channels - 1] * (1.0 / SENT_UNIT))

        zero = jnp.zeros((16, columns), jnp.float32)
        carry = ((zero,) * channels, jnp.full((16, columns), 1.0 / SENT_UNIT, jnp.float32))
        for position in range(bricks):
            carry = step(position, carry)
        for c in range(channels):
            out[c, at] = carry[0][c]


def blend(order, layers):
    bricks, channels, rows, columns = layers.shape
    block = pl.BlockSpec(memory_space=pltpu.VMEM)
    return pl.pallas_call(
        blend_kernel,
        out_shape=jax.ShapeDtypeStruct((channels, rows, columns), jnp.float32),
        in_specs=[pl.BlockSpec(memory_space=pltpu.SMEM), block],
        out_specs=block,
        compiler_params=pltpu.CompilerParams(vmem_limit_bytes=BLEND_LIMIT),
        name="blend",
    )(order, layers)


def shards(volume, occupied, sample_counts, depth_order, colors, density):
    slices, rows, columns = volume.shape
    bricks = lax.axis_size("view")
    bands = lax.axis_size("img")
    back = [(i + 1, i) for i in range(bricks - 1)]
    down = [(i, i + 1) for i in range(bands - 1)]
    up = [(i + 1, i) for i in range(bands - 1)]
    tiles_of = (occupied.reshape(-1), sample_counts.reshape(-1))
    density = density[None, :]
    low = lax.ppermute(volume[:, rows - 1], "img", down)
    high = lax.ppermute(volume[:, 0], "img", up)
    middle = march((1, 2), *tiles_of, volume, (), colors, density)
    low, high, middle = lax.optimization_barrier((low, high, middle))
    padding = jnp.zeros((SENT_ROWS - rows - 2, columns), volume.dtype)
    first = jnp.concatenate([volume[0], low[0:1], high[0:1], padding], axis=0)
    following = lax.ppermute(first, "view", back)
    outer = march((0, 3), *tiles_of, volume, (low, high), colors, density)
    partial = finish(*tiles_of, volume, (low, high), following, middle, outer, colors, density)
    layers = lax.all_to_all(partial, "view", 0, 0, tiled=True)
    return blend(depth_order, layers)


def solution(mesh):
    return jax.shard_map(
        shards,
        mesh=mesh,
        in_specs=(
            P("view", "img", None),
            P("view", "img", None),
            P("view", "img", None),
            P(),
            P(),
            P(),
        ),
        out_specs=P(None, "img", "view"),
        check_vma=False,
    )
```

```python
import functools

import jax
import jax.numpy as jnp
from jax import lax
from jax.experimental import pallas as pl
from jax.experimental.pallas import tpu as pltpu
from jax.sharding import PartitionSpec as P

TILE_COLS = 128
GROUP_ROWS = 8
SENT_ROWS = 48
UNROLL = 12
VMEM_LIMIT = 60 * 2**20
BLEND_LIMIT = 16 * 2**20
UNROLLS = (5, 6, 7, 8, 9, 10, 11, 12)
LOG2E = 1.4426950408889634
COLOR_UNIT = 4096.0
DENSITY_UNIT = 65536.0
ENTRY_SHIFT = 18
SENT_UNIT = 131070.0
SENT_ZERO = 32768

LANE_GATHER = lax.GatherDimensionNumbers(
    offset_dims=(),
    collapsed_slice_dims=(1,),
    start_index_map=(1,),
    operand_batching_dims=(0,),
    start_indices_batching_dims=(0,),
)


def looked_up(row, index):
    return lax.gather(
        row,
        index[..., None],
        LANE_GATHER,
        slice_sizes=(1, 1),
        mode=lax.GatherScatterMode.PROMISE_IN_BOUNDS,
    )


def tile_table(colors, density):
    shape = (GROUP_ROWS, TILE_COLS)
    table = []
    for channel in range(4):
        source = colors[channel : channel + 1] if channel < 3 else density[...]
        unit = COLOR_UNIT if channel < 3 else DENSITY_UNIT
        entry = jnp.broadcast_to((source.astype(jnp.float32) * unit).astype(jnp.int32), shape)
        second = pltpu.roll(entry, TILE_COLS - 1, 1)
        table.append((entry << ENTRY_SHIFT) | second)
    return table


def listed_by_samples(occupied, counts, ordered):
    slots = occupied.shape[0]
    tiles = [occupied[slot] for slot in range(slots)]
    samples = [counts[jnp.maximum(tile, 0)] for tile in tiles]
    keys = [
        jnp.where(tile >= 0, count * slots + slot, slots * 1024 + slot)
        for slot, (tile, count) in enumerate(zip(tiles, samples))
    ]
    listed = jnp.int32(0)
    ranks = [jnp.int32(slot) for slot in range(slots)]
    for slot in range(slots):
        for other in range(slot):
            moved = (keys[slot] < keys[other]).astype(jnp.int32)
            ranks[other] = ranks[other] + moved
            ranks[slot] = ranks[slot] - moved
    for slot in range(slots):
        ordered[ranks[slot]] = tiles[slot]
        listed = listed + (tiles[slot] >= 0).astype(jnp.int32)
    return listed


def samples_before_last(samples, slices):
    return ((slices - 1) * samples) // slices


def neighbours(tile, tiles):
    here = pl.multiple_of(tile * TILE_COLS, TILE_COLS)
    before = pl.multiple_of(jnp.maximum(tile - 1, 0) * TILE_COLS, TILE_COLS)
    after = pl.multiple_of(jnp.minimum(tile + 1, tiles - 1) * TILE_COLS, TILE_COLS)
    return before, here, after


def prepared(load, low_row, high_row, tile, tiles, groups_of, count):
    shape = (GROUP_ROWS, TILE_COLS)
    before, here, after = neighbours(tile, tiles)
    row_of = lax.broadcasted_iota(jnp.int32, shape, 0)
    lane_of = lax.broadcasted_iota(jnp.int32, shape, 1)

    def split(block):
        block = block.astype(jnp.float32)
        return [block[g * GROUP_ROWS : (g + 1) * GROUP_ROWS] for g in range(count)]

    parts, lefts, rights = split(load(here)), split(load(before)), split(load(after))
    result = {}
    for g in groups_of:
        part = parts[g]
        left = jnp.where(tile > 0, lefts[g], 0.0)
        right = jnp.where(tile < tiles - 1, rights[g], 0.0)
        left = pltpu.roll(jnp.where(lane_of == TILE_COLS - 1, left, part), 1, 1)
        right = pltpu.roll(jnp.where(lane_of == 0, right, part), TILE_COLS - 1, 1)
        above = pltpu.roll(parts[g - 1], 1, 0) if g > 0 else jnp.broadcast_to(low_row, shape)
        below = (
            pltpu.roll(parts[g + 1], GROUP_ROWS - 1, 0) if g < count - 1 else jnp.broadcast_to(high_row, shape)
        )
        above = jnp.where(row_of == 0, above, pltpu.roll(part, 1, 0))
        below = jnp.where(row_of == GROUP_ROWS - 1, below, pltpu.roll(part, GROUP_ROWS - 1, 0))
        across = below - above
        along = right - left
        result[g] = part * 0.5, (across * across + along * along) * (0.25 / 0.6) + (1.0 / 0.6)
    return result


def looked(half_value, gradient, table):
    level = 63.5 + 63.5 * jnp.tanh(half_value)
    index = level.astype(jnp.int32)
    second = level - index.astype(jnp.float32)
    first = 1.0 - second
    second = second.astype(jnp.bfloat16).astype(jnp.float32)
    first = first.astype(jnp.bfloat16).astype(jnp.float32)
    pairs = [looked_up(row, index) for row in table]
    shade = 1.0 - pl.reciprocal(gradient, approx=True)
    return first, second, shade, pairs


def composited(thick, sample, state):
    first, second, shade, pairs = sample
    uppers = [pair.astype(jnp.float32) for pair in pairs]
    lowers = [(pair << ENTRY_SHIFT).astype(jnp.float32) for pair in pairs]
    red, green, blue, remain = state
    remain_after = remain * jnp.exp2((first * uppers[3] + second * lowers[3]) * thick)
    weight = (remain - remain_after) * shade
    first = weight * first
    second = weight * second
    return (
        red + first * uppers[0] + second * lowers[0],
        green + first * uppers[1] + second * lowers[1],
        blue + first * uppers[2] + second * lowers[2],
        remain_after,
    )


def march_kernel(groups, edges, *refs):
    there = refs[: 5 + edges]
    out = refs[5 + edges]
    refs = refs[6 + edges :]
    if not edges:
        first, refs = refs[0], refs[1:]
    here = refs[: 5 + edges]
    halves, steps, grads, ordered, sems = refs[5 + edges :]
    occupied, counts, colors, density, cube = here[:5]
    if edges:
        low, high = here[5:]
    slices, rows, columns = there[4].shape
    targets = [*here[:4], cube.at[:, :, pl.ds(TILE_COLS, columns)], *here[5:]]
    copies = [pltpu.make_async_copy(source, target, sems.at[i]) for i, (source, target) in enumerate(zip(there, targets))]
    for copy in copies:
        copy.start()
    for end in (0, columns + TILE_COLS):
        cube[:, :, pl.ds(end, TILE_COLS)] = jnp.zeros((slices, rows, TILE_COLS), cube.dtype)
    tiles = columns // TILE_COLS
    count = rows // GROUP_ROWS
    shape = (GROUP_ROWS, TILE_COLS)
    for copy in copies[:4]:
        copy.wait()
    listed = listed_by_samples(occupied, counts, ordered)
    table = tile_table(colors, density)
    for copy in copies[4:]:
        copy.wait()
    if not edges:
        first_copy = pltpu.make_async_copy(
            cube.at[0, :, pl.ds(TILE_COLS, columns)], first.at[pl.ds(0, rows)], sems.at[5]
        )
        first_copy.start()

    lane_of = lax.broadcasted_iota(jnp.int32, shape, 1)

    def rows_of(g):
        return pl.ds((g + 1) * GROUP_ROWS, GROUP_ROWS)

    def prepare(tile, place):
        at = pl.multiple_of(tile * TILE_COLS, TILE_COLS)
        near = [pl.ds(pl.multiple_of(at + i * TILE_COLS, TILE_COLS), TILE_COLS) for i in range(3)]
        if edges:
            low_rows = low[:, pl.ds(at, TILE_COLS)].astype(jnp.float32) * 0.5
            high_rows = high[:, pl.ds(at, TILE_COLS)].astype(jnp.float32) * 0.5
        last_half, last_gradient = {}, {}
        for j in range(slices):
            left, block, right = [cube[j, :, span].astype(jnp.float32) for span in near]
            if edges:
                halves[place, j, GROUP_ROWS - 1 : GROUP_ROWS] = low_rows[j : j + 1]
                halves[place, j, rows + GROUP_ROWS : rows + GROUP_ROWS + 1] = high_rows[j : j + 1]
            for g in range(count):
                halves[place, j, rows_of(g)] = block[g * GROUP_ROWS : (g + 1) * GROUP_ROWS] * 0.5
            for i, g in enumerate(groups):
                part = slice(g * GROUP_ROWS, (g + 1) * GROUP_ROWS)
                half = block[part] * 0.5
                before = pltpu.roll(jnp.where(lane_of == TILE_COLS - 1, left[part], block[part]), 1, 1)
                after = pltpu.roll(jnp.where(lane_of == 0, right[part], block[part]), TILE_COLS - 1, 1)
                along = after - before
                above = halves[place, j, pl.ds((g + 1) * GROUP_ROWS - 1, GROUP_ROWS)]
                below = halves[place, j, pl.ds((g + 1) * GROUP_ROWS + 1, GROUP_ROWS)]
                across = below - above
                gradient = across * across * (1.0 / 0.6) + (along * along * (0.25 / 0.6) + (1.0 / 0.6))
                grads[place, 2 * j, i] = gradient
                if j > 0:
                    steps[place, j - 1, i] = half - last_half[g]
                    grads[place, 2 * j - 1, i] = gradient - last_gradient[g]
                last_half[g], last_gradient[g] = half, gradient

    def march_two(number, carry):
        two = [ordered[2 * number], ordered[2 * number + 1]]
        marched, spacing, thickness = [], [], []
        for place, tile in enumerate(two):
            samples = counts[tile]
            marched.append(samples_before_last(samples, slices))
            spacing.append(slices / samples.astype(jnp.float32))
            thickness.append(spacing[place] * (-LOG2E / (DENSITY_UNIT * (1 << ENTRY_SHIFT))))
            prepare(tile, place)

        def sampled(k, place):
            position = jnp.minimum((k + 1).astype(jnp.float32) * spacing[place], slices - 1.0)
            j = jnp.minimum(position.astype(jnp.int32), slices - 2)
            part = position - j.astype(jnp.float32)
            return [
                looked(
                    halves[place, j, rows_of(g)] + part * steps[place, j, i],
                    grads[place, 2 * j, i] + part * grads[place, 2 * j + 1, i],
                    table,
                )
                for i, g in enumerate(groups)
            ]

        longest = jnp.maximum(marched[0], marched[1])
        blocks = (longest + UNROLL - 1) // UNROLL
        size = (longest + blocks - 1) // blocks
        chains = [(place, i) for place in range(2) for i in range(len(groups))]

        def march_blocks(unroll):
            def march_block(number, states):
                states = list(states)
                base = number * unroll
                ready = [[sampled(base + u, place) for place in range(2)] for u in range(unroll)]
                for u in range(unroll):
                    thick = [jnp.where(base + u < marched[place], thickness[place], 0.0) for place in range(2)]
                    for c, (place, i) in enumerate(chains):
                        states[c] = composited(thick[place], ready[u][place][i], states[c])
                return tuple(states)

            zero = jnp.zeros(shape, jnp.float32)
            start = tuple((zero, zero, zero, jnp.ones(shape, jnp.float32)) for c in chains)
            states = lax.fori_loop(0, blocks, march_block, start)
            for c, (place, i) in enumerate(chains):
                for channel in range(4):
                    out[two[place], i, channel] = states[c][channel]

        for unroll in UNROLLS:
            at_least = unroll == UNROLLS[0]
            pl.when(size <= unroll if at_least else size == unroll)(functools.partial(march_blocks, unroll))
        return carry

    lax.fori_loop(0, listed // 2, march_two, 0)
    if not edges:
        first_copy.wait()


def held_here(value):
    space = pltpu.SMEM if value.dtype == jnp.int32 else pltpu.VMEM
    return space(value.shape, value.dtype)


def march(groups, occupied, counts, volume, edges, colors, density):
    slices, rows, columns = volume.shape
    arrays = (occupied, counts, colors, density, volume, *edges)
    tile = (len(groups), GROUP_ROWS, TILE_COLS)
    images = jax.ShapeDtypeStruct((columns // TILE_COLS, len(groups), 4, GROUP_ROWS, TILE_COLS), jnp.float32)
    place = pl.BlockSpec(memory_space=pltpu.VMEM)
    scratch = [held_here(value) for value in arrays]
    scratch[4] = pltpu.VMEM((slices, rows, columns + 2 * TILE_COLS), volume.dtype)
    return pl.pallas_call(
        functools.partial(march_kernel, groups, len(edges)),
        out_shape=images if edges else (images, jax.ShapeDtypeStruct((SENT_ROWS, columns), volume.dtype)),
        in_specs=[pl.BlockSpec(memory_space=pl.ANY)] * len(arrays),
        out_specs=place if edges else (place, pl.BlockSpec(memory_space=pl.ANY)),
        scratch_shapes=scratch
        + [
            pltpu.VMEM((2, slices, rows + 2 * GROUP_ROWS, TILE_COLS), jnp.float32),
            pltpu.VMEM((2, slices - 1, *tile), jnp.float32),
            pltpu.VMEM((2, 2 * slices - 1, *tile), jnp.float32),
            pltpu.SMEM(occupied.shape, jnp.int32),
            pltpu.SemaphoreType.DMA((len(arrays) + 1,)),
        ],
        compiler_params=pltpu.CompilerParams(vmem_limit_bytes=VMEM_LIMIT),
        cost_estimate=pl.CostEstimate(flops=8_000_000, bytes_accessed=16_000_000, transcendentals=2_000_000),
        name="march_edges" if edges else "march_middle",
    )(*arrays)


def finish_kernel(
    occupied_hbm,
    counts_hbm,
    colors_hbm,
    density_hbm,
    volume_hbm,
    low_hbm,
    high_hbm,
    following_hbm,
    middle_hbm,
    outer_hbm,
    out,
    occupied,
    counts,
    colors,
    density,
    own,
    low,
    high,
    following,
    middle,
    outer,
    sems,
):
    slices, rows, columns = volume_hbm.shape
    tiles = columns // TILE_COLS
    count = rows // GROUP_ROWS
    pairs = [
        (occupied_hbm, occupied),
        (counts_hbm, counts),
        (colors_hbm, colors),
        (density_hbm, density),
        (volume_hbm.at[pl.ds(slices - 1, 1)], own),
        (low_hbm, low),
        (high_hbm, high),
        (following_hbm, following),
        (middle_hbm, middle),
        (outer_hbm, outer),
    ]
    copies = [pltpu.make_async_copy(source, target, sems.at[i]) for i, (source, target) in enumerate(pairs)]
    for copy in copies:
        copy.start()
    out[...] = jnp.full(out.shape, -SENT_ZERO, jnp.int16)
    for copy in copies:
        copy.wait()
    table = tile_table(colors, density)
    listed = jnp.int32(0)
    for slot in range(tiles):
        listed = listed + (occupied[slot] >= 0).astype(jnp.int32)

    def finish_tile(tile):
        samples = counts[tile]
        marched = samples_before_last(samples, slices)
        here = neighbours(tile, tiles)[1]
        groups = tuple(range(count))
        low_rows = low[:, pl.ds(here, TILE_COLS)].astype(jnp.float32)
        high_rows = high[:, pl.ds(here, TILE_COLS)].astype(jnp.float32)
        next_edges = following[rows : rows + 2, pl.ds(here, TILE_COLS)].astype(jnp.float32)
        near = prepared(
            lambda start: own[0, :, pl.ds(start, TILE_COLS)],
            low_rows[slices - 1 : slices],
            high_rows[slices - 1 : slices],
            tile,
            tiles,
            groups,
            count,
        )
        far = prepared(
            lambda start: following[0:rows, pl.ds(start, TILE_COLS)],
            next_edges[0:1],
            next_edges[1:2],
            tile,
            tiles,
            groups,
            count,
        )
        spacing = slices / samples.astype(jnp.float32)
        thickness = spacing * (-LOG2E / (DENSITY_UNIT * (1 << ENTRY_SHIFT)))
        states = []
        for g in groups:
            source, i = (middle, g - 1) if 0 < g < count - 1 else (outer, 0 if g == 0 else 1)
            states.append(tuple(source[tile, i, channel] for channel in range(4)))
        for u in range(2):
            k = marched + u
            part = jnp.minimum((k + 1).astype(jnp.float32) * spacing - (slices - 1.0), 1.0)
            thick = jnp.where(k < samples, thickness, 0.0)
            for g in groups:
                half_value = near[g][0] + part * (far[g][0] - near[g][0])
                gradient = near[g][1] + part * (far[g][1] - near[g][1])
                states[g] = composited(thick, looked(half_value, gradient, table), states[g])
        for pair in range(count // 2):
            for channel in range(4):
                both = jnp.concatenate([states[2 * pair][channel], states[2 * pair + 1][channel]], axis=0)
                if channel == 3:
                    both = (1.0 - both) * SENT_UNIT
                else:
                    both = both * (SENT_UNIT / (COLOR_UNIT * (1 << ENTRY_SHIFT)))
                both = jnp.round(both).astype(jnp.int32) - SENT_ZERO
                out[tile, channel, pl.ds(2 * GROUP_ROWS * pair, 2 * GROUP_ROWS)] = both.astype(jnp.int16)

    def finish_two(number, carry):
        finish_tile(occupied[2 * number])
        finish_tile(occupied[2 * number + 1])
        return carry

    lax.fori_loop(0, listed // 2, finish_two, 0)


def finish(occupied, counts, volume, edges, following, middle, outer, colors, density):
    slices, rows, columns = volume.shape
    arrays = (occupied, counts, colors, density, volume, *edges, following, middle, outer)
    scratch = [held_here(value) for value in arrays]
    scratch[4] = pltpu.VMEM((1, rows, columns), volume.dtype)
    return pl.pallas_call(
        finish_kernel,
        out_shape=jax.ShapeDtypeStruct((columns // TILE_COLS, 4, rows, TILE_COLS), jnp.int16),
        in_specs=[pl.BlockSpec(memory_space=pl.ANY)] * len(arrays),
        out_specs=pl.BlockSpec(memory_space=pltpu.VMEM),
        scratch_shapes=scratch + [pltpu.SemaphoreType.DMA((len(arrays),))],
        compiler_params=pltpu.CompilerParams(vmem_limit_bytes=VMEM_LIMIT),
        name="finish",
    )(*arrays)


def blend_kernel(order, layers, out):
    bricks, channels, rows, columns = layers.shape
    for start in range(0, rows, 16):
        at = pl.ds(start, 16)

        def step(position, carry):
            image, remain = carry
            brick = order[position]
            chosen = [
                (layers[brick, c, at].astype(jnp.int32) + SENT_ZERO).astype(jnp.float32) for c in range(channels)
            ]
            image = tuple(image[c] + remain * chosen[c] for c in range(channels))
            return image, remain * (1.0 - chosen[channels - 1] * (1.0 / SENT_UNIT))

        zero = jnp.zeros((16, columns), jnp.float32)
        carry = ((zero,) * channels, jnp.full((16, columns), 1.0 / SENT_UNIT, jnp.float32))
        for position in range(bricks):
            carry = step(position, carry)
        for c in range(channels):
            out[c, at] = carry[0][c]


def blend(order, layers):
    bricks, channels, rows, columns = layers.shape
    block = pl.BlockSpec(memory_space=pltpu.VMEM)
    return pl.pallas_call(
        blend_kernel,
        out_shape=jax.ShapeDtypeStruct((channels, rows, columns), jnp.float32),
        in_specs=[pl.BlockSpec(memory_space=pltpu.SMEM), block],
        out_specs=block,
        compiler_params=pltpu.CompilerParams(vmem_limit_bytes=BLEND_LIMIT),
        name="blend",
    )(order, layers)


def shards(volume, occupied, sample_counts, depth_order, colors, density):
    slices, rows, columns = volume.shape
    bricks = lax.axis_size("view")
    bands = lax.axis_size("img")
    back = [(i + 1, i) for i in range(bricks - 1)]
    down = [(i, i + 1) for i in range(bands - 1)]
    up = [(i + 1, i) for i in range(bands - 1)]
    tiles_of = (occupied.reshape(-1), sample_counts.reshape(-1))
    density = density[None, :]
    low = lax.ppermute(volume[:, rows - 1], "img", down)
    high = lax.ppermute(volume[:, 0], "img", up)
    middle, first = march((1, 2), *tiles_of, volume, (), colors, density)
    low, high, middle, first = lax.optimization_barrier((low, high, middle, first))
    padding = jnp.zeros((SENT_ROWS - rows - 2, columns), volume.dtype)
    beside = jnp.concatenate([low[0:1], high[0:1], padding], axis=0)
    first = lax.dynamic_update_slice(first, beside, (rows, 0))
    following = lax.ppermute(first, "view", back)
    outer = march((0, 3), *tiles_of, volume, (low, high), colors, density)
    partial = finish(*tiles_of, volume, (low, high), following, middle, outer, colors, density)
    layers = lax.all_to_all(partial, "view", 0, 0, tiled=True)
    return blend(depth_order, layers)


def solution(mesh):
    return jax.shard_map(
        shards,
        mesh=mesh,
        in_specs=(
            P("view", "img", None),
            P("view", "img", None),
            P("view", "img", None),
            P(),
            P(),
            P(),
        ),
        out_specs=P(None, "img", "view"),
        check_vma=False,
    )
```
